32 devices in a mesh: section: 2 (over core), grp: 4 (over y, x), tile: 4 (over z).
Axes of the slice: x: 2, y: 2, z: 4, core: 2. Of those that a mesh axis runs over, the one named last changes fastest.
Arguments:
- latent: bfloat16 [4, 4, 16, 1536], P('grp', 'section', 'tile'), may hold values from -6 to 6
- latent_mean: float32 [16], replicated, may hold values from -1 to 1
- latent_scale: float32 [16], replicated, may hold values from 0.5 to 3
- cache_latent: bfloat16 [4, 2, 16, 1536], P('grp', None, 'tile', 'section'), may hold values from -9 to 9
- input_weight: bfloat16 [3, 3, 3, 16, 384], replicated, may hold values from -0.3125 to 0.3125
- mid_gain: float32 [384], replicated, may hold values from 0.25 to 1.75
- mid_cache: bfloat16 [4, 2, 16, 96, 384], P('grp', None, 'tile', 'section'), may hold values from -5 to 5
- mid_weight: bfloat16 [3, 3, 3, 384, 384], P(None, None, None, None, 'tile'), may hold values from -0.0625 to 0.0625
- up_weight: bfloat16 [3, 3, 384, 768], replicated, may hold values from -0.109375 to 0.109375
Outputs:
- upsampled: bfloat16 [4, 4, 32, 192, 192], P('grp', None, 'tile', 'section')
The draws below stay inside these ranges and needn't reach their ends.
All inputs are finite; a program needn't handle non-finite values.
Results may differ from the reference program's by a relative error of at most 0.0064.
Values may be sent and summed in bfloat16 or wider, within the bound.
A program may use at most 128 MiB of HBM per device.

```python
import math
import jax
import jax.numpy as jnp
from jax import lax

CL = 16
C = 384
CU = 192
FRAMES = 4
W = 96
H = 16
GROUPS = 4


def steps_of(rng, dims, shards, least, largest):
    def one(position, shards_of):
        steps = jax.random.uniform(jax.random.fold_in(jax.random.fold_in(rng, 6), position), (shards_of,), jnp.float32, least / len(shards), largest / len(shards))
        return jnp.repeat(jnp.exp(steps), dims[position] // shards_of).reshape((-1,) + (1,) * (len(dims) - position - 1))

    level = one(*shards[0])
    for cut in shards[1:]:
        level = level * one(*cut)
    return level


def normal_values(stream_key, shape, width, most, cuts=(), held_as=jnp.bfloat16):
    array = jax.random.normal(stream_key, shape, jnp.float32) * width
    if len(cuts) > 0:
        array = steps_of(stream_key, shape, cuts, -0.22, 0.18) * array
    return jnp.clip(array, min=-most, max=most).astype(held_as)


def setup_inputs(seed: int = 0) -> dict:
    streams_of = jax.random.split(jax.random.key(seed), 10)
    return {
        "latent": normal_values(streams_of[0], (GROUPS, FRAMES, H, W * CL), 1.0, 6.0, ((0, 4), (1, 2), (2, 4))),
        "latent_mean": jnp.clip(jax.random.uniform(streams_of[1], (CL,), jnp.float32, -1.0, 1.0), -1.0, 1.0),
        "latent_scale": jnp.clip(jnp.exp(jax.random.uniform(streams_of[2], (CL,), jnp.float32, math.log(0.5), math.log(3.0))), 0.5, 3.0),
        "cache_latent": normal_values(streams_of[3], (GROUPS, 2, H, W * CL), 1.5, 9.0, ((0, 4), (2, 4), (3, 2))),
        "input_weight": normal_values(streams_of[4], (3, 3, 3, CL, C), (27 * CL) ** -0.5, 0.3125),
        "mid_gain": jnp.clip(1.0 + 0.15 * jax.random.normal(streams_of[5], (C,), jnp.float32), 0.25, 1.75),
        "mid_cache": normal_values(streams_of[6], (GROUPS, 2, H, W, C), 0.8, 5.0, ((0, 4), (2, 4), (3, 2))),
        "mid_weight": normal_values(streams_of[7], (3, 3, 3, C, C), (27 * C) ** -0.5, 0.0625, ((4, 4),)),
        "up_weight": normal_values(streams_of[8], (3, 3, C, 4 * CU), (9 * C) ** -0.5, 0.109375),
    }


def causal_conv(inputs, kernel):
    return lax.conv_general_dilated(inputs[None], kernel, (1, 1, 1), [(0, 0), (1, 1), (1, 1)], dimension_numbers=('NDHWC', 'DHWIO', 'NDHWC'), preferred_element_type=jnp.float32)[0]

def activate(values, gain_vector):
    floats = values.astype(jnp.float32)
    inverse_rms = lax.rsqrt(lax.optimization_barrier(jnp.mean(floats * floats, axis=-1, keepdims=True)) + 1e-06)
    return jax.nn.silu(floats * inverse_rms * gain_vector).astype(jnp.bfloat16)

def to_pixels(phases, out_channels):
    frame_count, row_count, col_count, _ = phases.shape
    split = phases.reshape(frame_count, row_count, col_count, 2, 2, out_channels)
    return jnp.transpose(split, (0, 1, 3, 2, 4, 5)).reshape(frame_count, 2 * row_count, 2 * col_count, out_channels)

def reference(latent, latent_mean, latent_scale, cache_latent, input_weight, mid_gain, mid_cache, mid_weight, up_weight):

    def window(packed):
        latent_tile, cache_tile, mid_tile = packed
        scaled = (latent_tile.astype(jnp.float32).reshape(FRAMES, H, W, CL) * latent_scale + latent_mean).astype(jnp.bfloat16)
        joined = jnp.concatenate([cache_tile.reshape(2, H, W, CL), scaled], axis=0)
        features = causal_conv(joined, input_weight).astype(jnp.bfloat16)
        acted = activate(features, mid_gain)
        stacked = jnp.concatenate([mid_tile, acted], axis=0)
        mixed = (features.astype(jnp.float32) + causal_conv(stacked, mid_weight)).astype(jnp.bfloat16)
        phases = lax.conv_general_dilated(mixed, up_weight, (1, 1), [(1, 1), (1, 1)], dimension_numbers=('NHWC', 'HWIO', 'NHWC'), preferred_element_type=jnp.float32).astype(jnp.bfloat16)
        return to_pixels(phases, CU)
    return lax.map(window, (latent, cache_latent, mid_cache))
```

```python
import functools

import jax
import jax.numpy as jnp
from jax import lax
from jax.experimental import pallas as pl
from jax.experimental.pallas import tpu as pltpu
from jax.sharding import PartitionSpec as P

MESH = pl.DeviceIdType.MESH
PIECES = 8


def exchange_kernel(
    n, w_ref, lat_ref, cl_ref, mc_ref,
    g_ref, latx_ref, clx_ref, mcv_ref, mch_ref,
    own_sem, hs_sem, hr_sem, zs_sem, zr_sem, ps_sem, pr_sem, ss_sem, sr_sem,
):
    s = lax.axis_index("section")
    g = lax.axis_index("grp")
    t = lax.axis_index("tile")
    gx = g + 1 - 2 * (g % 2)
    gy = g + 2 - 4 * ((g // 2) % 2)
    gd = gx + 2 - 4 * ((gx // 2) % 2)
    o = 1 - s
    chunks = w_ref.shape[0]
    per = chunks // PIECES
    half = per // 2
    rest = chunks - per * PIECES
    has = {-1: t > 0, 0: None, 1: t < n - 1}

    def dev(ds=0, group=None, dt=0):
        return {
            "section": o if ds else s,
            "grp": g if group is None else group,
            "tile": t + dt,
        }

    def guarded(cond, fn):
        if cond is None:
            fn()
        else:
            pl.when(cond)(fn)

    partners = [(dev(1), None), (dev(0, gx), None), (dev(0, gy), None)]
    for dt in (-1, 1):
        partners += [(dev(0, None, dt), has[dt]), (dev(1, None, dt), has[dt])]
    barrier = pltpu.get_barrier_semaphore()
    for target, cond in partners:
        guarded(
            cond,
            functools.partial(
                pl.semaphore_signal, barrier, inc=1, device_id=target, device_id_type=MESH
            ),
        )
    own = [
        pltpu.make_async_copy(w_ref, g_ref.at[:, t], own_sem.at[0]),
        pltpu.make_async_copy(lat_ref, latx_ref.at[1, s], own_sem.at[1]),
        pltpu.make_async_copy(cl_ref, clx_ref.at[1, s], own_sem.at[2]),
    ]
    for copy in own:
        copy.start()
    pl.semaphore_wait(barrier, 3 + 2 * (jnp.minimum(t, 1) + jnp.minimum(n - 1 - t, 1)))

    def remote(src, dst, ssem, rsem, target):
        return pltpu.make_async_remote_copy(
            src_ref=src, dst_ref=dst, send_sem=ssem, recv_sem=rsem,
            device_id=target, device_id_type=MESH,
        )

    rows, cols = mc_ref.shape[1], mc_ref.shape[2]
    edge = pl.multiple_of((cols - 16) * o, 16)
    halo = []
    for dt in (-1, 0, 1):
        first = 0 if dt < 0 else rows - 2
        for ds in (0, 1):
            if (ds, dt) == (0, 0):
                continue
            k = len(halo)
            base = 3 * k
            sems = [(hs_sem.at[base + j], hr_sem.at[base + j]) for j in range(3)]
            target = dev(ds, None, dt)
            back = len(halo)
            copies = [
                (lat_ref, latx_ref.at[1 - dt, s]),
                (cl_ref, clx_ref.at[1 - dt, s]),
            ]
            if ds == 0:
                copies.append((mc_ref.at[:, pl.ds(first, 2)], mcv_ref.at[(1 - dt) // 2]))
            elif dt == 0:
                copies.append((mc_ref.at[:, :, pl.ds(edge, 16)], mch_ref.at[1]))
            else:
                copies.append(
                    (
                        mc_ref.at[:, pl.ds(first, 2), pl.ds(edge, 16)],
                        mch_ref.at[1 - dt, :, pl.ds(0, 2)],
                    )
                )
            halo.append(
                (
                    dt,
                    ds,
                    [remote(a, b, x, y, target) for (a, b), (x, y) in zip(copies, sems)],
                )
            )

    events = []
    for i in range(n - 1):
        for d in (0, 1):
            if d == 0:
                events.append((i, d, t - 1 - i, t - 1 - i >= 0))
            else:
                events.append((i, d, t + 1 + i, t + 1 + i <= n - 1))

    def block(group, part, u):
        begin = (2 * (group % 4) + s) * per
        if part == 0:
            return g_ref.at[pl.ds(begin, half), u]
        if part == 1:
            return g_ref.at[pl.ds(begin + half, per - half), u]
        return g_ref.at[pl.ds(begin, per), u]

    tail = pl.ds(per * PIECES, rest)

    def z_copies(i, d, u, first):
        begin = (2 * (g % 4) + s) * per
        dt = 1 if d == 0 else -1
        e = 2 * i + d
        src_a = w_ref.at[pl.ds(begin, per)] if first else block(g, 2, u)
        src_b = w_ref.at[tail] if first else g_ref.at[tail, u]
        target = dev(0, None, dt)
        return [
            remote(src_a, block(g, 2, u), zs_sem.at[2 * e], zr_sem.at[2 * e], target),
            remote(src_b, g_ref.at[tail, u], zs_sem.at[2 * e + 1], zr_sem.at[2 * e + 1], target),
        ]

    def d_copies(e, u):
        def one(k, group, part, to):
            b = block(group, part, u)
            return remote(b, b, ps_sem.at[6 * e + k], pr_sem.at[6 * e + k], dev(0, to))

        first = [one(0, g, 0, gx), one(1, g, 1, gy)]
        second = [one(2, g, 0, gy), one(3, gx, 0, gy), one(4, g, 1, gx), one(5, gy, 1, gx)]
        return first, second

    def s_copies(e, u):
        plan = [(g, 2), (gx, 0), (gy, 1), (gy, 0), (gd, 0), (gx, 1), (gd, 1)]
        made = []
        for k, (group, part) in enumerate(plan):
            b = block(group, part, u)
            made.append(remote(b, b, ss_sem.at[7 * e + k], sr_sem.at[7 * e + k], dev(1)))
        return made

    def begin_z(i, d, u, valid, first):
        dt = 1 if d == 0 else -1

        def go():
            for copy in z_copies(i, d, u, first):
                copy.start()

        pl.when(jnp.logical_and(valid, has[dt]))(go)

    def end_z(i, d, u, valid):
        dt = 1 if d == 0 else -1

        def go():
            for copy in z_copies(i, d, u, i == 0):
                copy.wait_send()

        pl.when(jnp.logical_and(valid, has[dt]))(go)

    begin_z(0, 0, t, t >= 0, True)
    begin_z(0, 1, t, t >= 0, True)
    for dt, ds, copies in halo:
        def go(copies=copies):
            for copy in copies:
                copy.start()
        guarded(has[dt], go)

    def arrive(e, i, d, u):
        for copy in z_copies(i, d, u, False):
            copy.wait_recv()

    def stage_a(i, d, u, valid):
        e = 2 * i + d

        def go():
            arrive(e, i, d, u)
            for copy in d_copies(e, u)[0]:
                copy.start()
            s_copies(e, u)[0].start()

        pl.when(valid)(go)
        if i + 1 < n - 1:
            begin_z(i + 1, d, u, valid, False)

    def stage_b(i, d, u, valid):
        e = 2 * i + d

        def go():
            first, second = d_copies(e, u)
            sib = s_copies(e, u)
            first[0].wait_recv()
            second[0].start()
            second[1].start()
            sib[1].start()
            first[1].wait_recv()
            second[2].start()
            second[3].start()
            sib[2].start()

        pl.when(valid)(go)

    def stage_c(i, d, u, valid):
        e = 2 * i + d

        def go():
            _, second = d_copies(e, u)
            sib = s_copies(e, u)
            for k in range(4):
                second[k].wait_recv()
                sib[3 + k].start()

        pl.when(valid)(go)

    for slot in range(n + 1):
        for stage, lag in ((stage_a, 0), (stage_b, 1), (stage_c, 2)):
            i = slot - lag
            if 0 <= i < n - 1:
                for event in events[2 * i : 2 * i + 2]:
                    stage(*event)

    for copy in own:
        copy.wait()
    for dt, ds, copies in halo:
        guarded(has[dt], lambda copies=copies: [c.wait_send() for c in copies] and None)
    order = {(dt, ds): copies for dt, ds, copies in halo}
    for (dt, ds), copies in order.items():
        guarded(has[-dt], lambda copies=copies: [c.wait_recv() for c in copies] and None)
    for i, d, u, valid in events:
        e = 2 * i + d

        def finish(e=e, u=u):
            first, second = d_copies(e, u)
            for copy in first + second:
                copy.wait_send()
            for copy in s_copies(e, u):
                copy.wait()

        pl.when(valid)(finish)
        sent = t - i if d == 0 else t + i
        end_z(i, d, sent, sent >= 0 if d == 0 else sent <= n - 1)


def exchange(n, weights, latent, cache_latent, mid_cache):
    chunks, cw, lanes = weights.shape
    frames, rows, cols, channels = mid_cache.shape
    dt = weights.dtype
    shape = jax.ShapeDtypeStruct
    events = 2 * (n - 1)
    dma = lambda k: pltpu.SemaphoreType.DMA((k,))
    return pl.pallas_call(
        functools.partial(exchange_kernel, n),
        out_shape=(
            shape((chunks, n, cw, lanes), dt),
            shape((3, 2) + latent.shape, dt),
            shape((3, 2) + cache_latent.shape, dt),
            shape((2, frames, 2, cols, channels), dt),
            shape((3, frames, rows, 16, channels), dt),
        ),
        in_specs=[pl.BlockSpec(memory_space=pl.ANY)] * 4,
        out_specs=[pl.BlockSpec(memory_space=pl.ANY)] * 5,
        scratch_shapes=[
            dma(3), dma(15), dma(15), dma(2 * events), dma(2 * events),
            dma(6 * events), dma(6 * events), dma(7 * events), dma(7 * events),
        ],
        compiler_params=pltpu.CompilerParams(collective_id=0, has_side_effects=True),
    )(weights, latent, cache_latent, mid_cache)


def activate(values, gain_vector):
    floats = values.astype(jnp.float32)
    inverse_rms = lax.rsqrt(jnp.mean(floats * floats, axis=-1, keepdims=True) + 1e-06)
    return jax.nn.silu(floats * inverse_rms * gain_vector).astype(jnp.bfloat16)


def to_pixels(phases, out_channels):
    frame_count, row_count, col_count, _ = phases.shape
    split = phases.reshape(frame_count, row_count, col_count, 2, 2, out_channels)
    return jnp.transpose(split, (0, 1, 3, 2, 4, 5)).reshape(
        frame_count, 2 * row_count, 2 * col_count, out_channels
    )


def inside(start, count, limit):
    index = start + jnp.arange(count)
    return jnp.logical_and(index >= 0, index < limit)


def mid_conv(stacked, weights):
    kernel = weights.reshape(3, 3, 3, 3, -1, weights.shape[-1])
    kernel = jnp.transpose(kernel, (0, 1, 2, 3, 5, 4))
    kernel = kernel.reshape(3, 3, 3, -1, kernel.shape[-1])
    return lax.conv_general_dilated(
        stacked[None], kernel, (1, 1, 1), [(0, 0)] * 3,
        dimension_numbers=("NDHWC", "DHWIO", "NDHWC"),
        preferred_element_type=jnp.float32,
    )[0]


def local(
    n, latent, latent_mean, latent_scale, cache_latent, input_weight,
    mid_gain, mid_cache, mid_weight, up_weight,
):
    s = lax.axis_index("section")
    t = lax.axis_index("tile")
    channels = latent_mean.shape[0]
    mid = input_weight.shape[-1]
    cw = mid_weight.shape[-1]
    lanes = 128
    _, rows, cols, _ = mid_cache.shape[1:]
    shard = mid_weight.reshape(-1, lanes, cw).transpose(0, 2, 1)
    gathered, latx, clx, mcv, mch = exchange(
        n, shard, latent[0], cache_latent[0], mid_cache[0]
    )
    width = latx.shape[-1]
    frames = 2 * latx.shape[2]
    near = latx.transpose(1, 2, 0, 3, 4).reshape(frames, 3 * rows, width)[:, rows - 3 : 2 * rows + 3]
    repeats = width // channels
    scaled = (
        near.astype(jnp.float32) * jnp.tile(latent_scale, repeats) + jnp.tile(latent_mean, repeats)
    ).astype(jnp.bfloat16)
    cached = clx.transpose(2, 0, 3, 1, 4).reshape(clx.shape[2], 3 * rows, width)
    cached = cached[:, rows - 3 : 2 * rows + 3]
    joined = jnp.concatenate([cached, scaled], axis=0)
    joined = jnp.where(inside(t * rows - 3, rows + 6, n * rows)[:, None], joined, 0)
    joined = jnp.pad(joined, ((0, 0), (0, 0), (3 * channels, 3 * channels)))
    joined = lax.dynamic_slice_in_dim(joined, s * cols * channels, (cols + 6) * channels, axis=2)
    joined = joined.reshape(joined.shape[0], rows + 6, cols + 6, channels)
    features = lax.conv_general_dilated(
        joined[None], input_weight, (1, 1, 1), [(0, 0)] * 3,
        dimension_numbers=("NDHWC", "DHWIO", "NDHWC"),
        preferred_element_type=jnp.float32,
    )[0].astype(jnp.bfloat16)
    sided = jnp.concatenate([mch[0, :, :2], mch[1], mch[2, :, :2]], axis=1)
    sided = lax.dynamic_slice_in_dim(sided, 14 * s, 2, axis=2)
    centre = jnp.concatenate([mcv[0], mid_cache[0], mcv[1]], axis=1)
    cache = jnp.concatenate([sided, centre, sided], axis=2)
    stacked = jnp.concatenate([cache, activate(features, mid_gain)], axis=0)
    row_ok = inside(t * rows - 2, rows + 4, n * rows)[:, None, None]
    col_ok = inside(s * cols - 2, cols + 4, 2 * cols)[:, None]
    stacked = jnp.where(jnp.logical_and(row_ok, col_ok), stacked, 0)
    branch = mid_conv(stacked, gathered.reshape(gathered.shape[0], mid, lanes))
    mixed = features[:, 1:-1, 1:-1].astype(jnp.float32) + branch
    keep = jnp.logical_and(row_ok, col_ok)[1:-1, 1:-1]
    mixed = jnp.where(keep, mixed, 0).astype(jnp.bfloat16)
    phases = lax.conv_general_dilated(
        mixed, up_weight, (1, 1), [(0, 0), (0, 0)],
        dimension_numbers=("NHWC", "HWIO", "NHWC"),
        preferred_element_type=jnp.float32,
    ).astype(jnp.bfloat16)
    return to_pixels(phases, up_weight.shape[3] // 4)[None]


def solution(mesh):
    return jax.shard_map(
        functools.partial(local, mesh.shape["tile"]),
        mesh=mesh,
        in_specs=(
            P("grp", "section", "tile", None),
            P(),
            P(),
            P("grp", None, "tile", "section"),
            P(),
            P(),
            P("grp", None, "tile", "section", None),
            P(None, None, None, None, "tile"),
            P(),
        ),
        out_specs=P("grp", None, "tile", "section", None),
        check_vma=False,
    )
```

```python
import functools

import jax
import jax.numpy as jnp
from jax import lax
from jax.experimental import pallas as pl
from jax.experimental.pallas import tpu as pltpu
from jax.sharding import PartitionSpec as P

MESH = pl.DeviceIdType.MESH
PIECES = 8


def exchange_kernel(
    n, w_ref, lat_ref, cl_ref, mc_ref,
    g_ref, latx_ref, clx_ref, mcv_ref, mch_ref,
    own_sem, hs_sem, hr_sem, zs_sem, zr_sem, ps_sem, pr_sem, ss_sem, sr_sem,
):
    s = lax.axis_index("section")
    g = lax.axis_index("grp")
    t = lax.axis_index("tile")
    gx = g + 1 - 2 * (g % 2)
    gy = g + 2 - 4 * ((g // 2) % 2)
    gd = gx + 2 - 4 * ((gx // 2) % 2)
    o = 1 - s
    chunks = w_ref.shape[0]
    per = chunks // PIECES
    half = per // 2
    rest = chunks - per * PIECES
    has = {-1: t > 0, 0: None, 1: t < n - 1}

    def dev(ds=0, group=None, dt=0):
        return {
            "section": o if ds else s,
            "grp": g if group is None else group,
            "tile": t + dt,
        }

    def guarded(cond, fn):
        if cond is None:
            fn()
        else:
            pl.when(cond)(fn)

    partners = [(dev(1), None), (dev(0, gx), None), (dev(0, gy), None)]
    for dt in (-1, 1):
        partners += [(dev(0, None, dt), has[dt]), (dev(1, None, dt), has[dt])]
    barrier = pltpu.get_barrier_semaphore()
    for target, cond in partners:
        guarded(
            cond,
            functools.partial(
                pl.semaphore_signal, barrier, inc=1, device_id=target, device_id_type=MESH
            ),
        )
    own = [
        pltpu.make_async_copy(w_ref, g_ref.at[:, t], own_sem.at[0]),
        pltpu.make_async_copy(lat_ref, latx_ref.at[1, s], own_sem.at[1]),
        pltpu.make_async_copy(cl_ref, clx_ref.at[1, s], own_sem.at[2]),
    ]
    for copy in own:
        copy.start()
    pl.semaphore_wait(barrier, 3 + 2 * (jnp.minimum(t, 1) + jnp.minimum(n - 1 - t, 1)))

    def remote(src, dst, ssem, rsem, target):
        return pltpu.make_async_remote_copy(
            src_ref=src, dst_ref=dst, send_sem=ssem, recv_sem=rsem,
            device_id=target, device_id_type=MESH,
        )

    rows, cols = mc_ref.shape[1], mc_ref.shape[2]
    edge = pl.multiple_of((cols - 16) * o, 16)
    halo = []
    for dt in (-1, 0, 1):
        first = 0 if dt < 0 else rows - 2
        for ds in (0, 1):
            if (ds, dt) == (0, 0):
                continue
            k = len(halo)
            base = 3 * k
            sems = [(hs_sem.at[base + j], hr_sem.at[base + j]) for j in range(3)]
            target = dev(ds, None, dt)
            back = len(halo)
            copies = [
                (lat_ref, latx_ref.at[1 - dt, s]),
                (cl_ref, clx_ref.at[1 - dt, s]),
            ]
            if ds == 0:
                copies.append((mc_ref.at[:, pl.ds(first, 2)], mcv_ref.at[(1 - dt) // 2]))
            elif dt == 0:
                copies.append((mc_ref.at[:, :, pl.ds(edge, 16)], mch_ref.at[1]))
            else:
                copies.append(
                    (
                        mc_ref.at[:, pl.ds(first, 2), pl.ds(edge, 16)],
                        mch_ref.at[1 - dt, :, pl.ds(0, 2)],
                    )
                )
            halo.append(
                (
                    dt,
                    ds,
                    [remote(a, b, x, y, target) for (a, b), (x, y) in zip(copies, sems)],
                )
            )

    events = []
    for i in range(n - 1):
        for d in (0, 1):
            if d == 0:
                events.append((i, d, t - 1 - i, t - 1 - i >= 0))
            else:
                events.append((i, d, t + 1 + i, t + 1 + i <= n - 1))

    def block(group, part, u):
        begin = (2 * (group % 4) + s) * per
        if part == 0:
            return g_ref.at[pl.ds(begin, half), u]
        if part == 1:
            return g_ref.at[pl.ds(begin + half, per - half), u]
        return g_ref.at[pl.ds(begin, per), u]

    tail = pl.ds(per * PIECES, rest)

    def z_copies(i, d, u, first):
        begin = (2 * (g % 4) + s) * per
        dt = 1 if d == 0 else -1
        e = 2 * i + d
        src_a = w_ref.at[pl.ds(begin, per)] if first else block(g, 2, u)
        src_b = w_ref.at[tail] if first else g_ref.at[tail, u]
        target = dev(0, None, dt)
        return [
            remote(src_a, block(g, 2, u), zs_sem.at[2 * e], zr_sem.at[2 * e], target),
            remote(src_b, g_ref.at[tail, u], zs_sem.at[2 * e + 1], zr_sem.at[2 * e + 1], target),
        ]

    def d_copies(e, u):
        def one(k, group, part, to):
            b = block(group, part, u)
            return remote(b, b, ps_sem.at[6 * e + k], pr_sem.at[6 * e + k], dev(0, to))

        first = [one(0, g, 0, gx), one(1, g, 1, gy)]
        second = [one(2, g, 0, gy), one(3, gx, 0, gy), one(4, g, 1, gx), one(5, gy, 1, gx)]
        return first, second

    def s_copies(e, u):
        plan = [(g, 2), (gx, 0), (gy, 1), (gy, 0), (gd, 0), (gx, 1), (gd, 1)]
        made = []
        for k, (group, part) in enumerate(plan):
            b = block(group, part, u)
            made.append(remote(b, b, ss_sem.at[7 * e + k], sr_sem.at[7 * e + k], dev(1)))
        return made

    def begin_z(i, d, u, valid, first):
        dt = 1 if d == 0 else -1

        def go():
            for copy in z_copies(i, d, u, first):
                copy.start()

        pl.when(jnp.logical_and(valid, has[dt]))(go)

    def end_z(i, d, u, valid):
        dt = 1 if d == 0 else -1

        def go():
            for copy in z_copies(i, d, u, i == 0):
                copy.wait_send()

        pl.when(jnp.logical_and(valid, has[dt]))(go)

    begin_z(0, 0, t, t >= 0, True)
    begin_z(0, 1, t, t >= 0, True)
    for dt, ds, copies in halo:
        def go(copies=copies):
            for copy in copies:
                copy.start()
        guarded(has[dt], go)

    def arrive(e, i, d, u):
        for copy in z_copies(i, d, u, False):
            copy.wait_recv()

    def stage_a(i, d, u, valid):
        e = 2 * i + d

        def go():
            arrive(e, i, d, u)
            for copy in d_copies(e, u)[0]:
                copy.start()
            s_copies(e, u)[0].start()

        pl.when(valid)(go)
        if i + 1 < n - 1:
            begin_z(i + 1, d, u, valid, False)

    def stage_b(i, d, u, valid):
        e = 2 * i + d

        def go():
            first, second = d_copies(e, u)
            sib = s_copies(e, u)
            first[0].wait_recv()
            second[0].start()
            second[1].start()
            sib[1].start()
            first[1].wait_recv()
            second[2].start()
            second[3].start()
            sib[2].start()

        pl.when(valid)(go)

    def stage_c(i, d, u, valid):
        e = 2 * i + d

        def go():
            _, second = d_copies(e, u)
            sib = s_copies(e, u)
            for k in range(4):
                second[k].wait_recv()
                sib[3 + k].start()

        pl.when(valid)(go)

    for slot in range(n + 1):
        for stage, lag in ((stage_a, 0), (stage_b, 1), (stage_c, 2)):
            i = slot - lag
            if 0 <= i < n - 1:
                for event in events[2 * i : 2 * i + 2]:
                    stage(*event)

    for copy in own:
        copy.wait()
    for dt, ds, copies in halo:
        guarded(has[dt], lambda copies=copies: [c.wait_send() for c in copies] and None)
    order = {(dt, ds): copies for dt, ds, copies in halo}
    for (dt, ds), copies in order.items():
        guarded(has[-dt], lambda copies=copies: [c.wait_recv() for c in copies] and None)
    for i, d, u, valid in events:
        e = 2 * i + d

        def finish(e=e, u=u):
            first, second = d_copies(e, u)
            for copy in first + second:
                copy.wait_send()
            for copy in s_copies(e, u):
                copy.wait()

        pl.when(valid)(finish)
        sent = t - i if d == 0 else t + i
        end_z(i, d, sent, sent >= 0 if d == 0 else sent <= n - 1)


def exchange(n, weights, latent, cache_latent, mid_cache):
    chunks, cw, lanes = weights.shape
    frames, rows, cols, channels = mid_cache.shape
    dt = weights.dtype
    shape = jax.ShapeDtypeStruct
    events = 2 * (n - 1)
    dma = lambda k: pltpu.SemaphoreType.DMA((k,))
    return pl.pallas_call(
        functools.partial(exchange_kernel, n),
        out_shape=(
            shape((chunks, n, cw, lanes), dt),
            shape((3, 2) + latent.shape, dt),
            shape((3, 2) + cache_latent.shape, dt),
            shape((2, frames, 2, cols, channels), dt),
            shape((3, frames, rows, 16, channels), dt),
        ),
        in_specs=[pl.BlockSpec(memory_space=pl.ANY)] * 4,
        out_specs=[pl.BlockSpec(memory_space=pl.ANY)] * 5,
        scratch_shapes=[
            dma(3), dma(15), dma(15), dma(2 * events), dma(2 * events),
            dma(6 * events), dma(6 * events), dma(7 * events), dma(7 * events),
        ],
        compiler_params=pltpu.CompilerParams(collective_id=0, has_side_effects=True),
    )(weights, latent, cache_latent, mid_cache)


def activate(values, gain_vector):
    floats = values.astype(jnp.float32)
    inverse_rms = lax.rsqrt(jnp.mean(floats * floats, axis=-1, keepdims=True) + 1e-06)
    return jax.nn.silu(floats * inverse_rms * gain_vector).astype(jnp.bfloat16)


def inside(start, count, limit):
    index = start + jnp.arange(count)
    return jnp.logical_and(index >= 0, index < limit)


def convs_kernel(
    x_ref, feat_ref, mask_ref, w_ref, u_ref, out_ref, xs_ref, acc_ref, mx_ref, up_ref, tmp_ref
):
    step = pl.program_id(0)
    total, tall, wide, mid = x_ref.shape
    frames, inner = total - 2, tall - 2
    rows = inner - 2
    cols = out_ref.shape[2] // 2
    out_channels = out_ref.shape[3]
    pair = 2

    @pl.when(step == 0)
    def _():
        acc_ref[...] = jnp.zeros_like(acc_ref)

        @pl.loop(0, total)
        def _(f):
            value = x_ref[f].reshape(tall * wide, mid).astype(jnp.float32)
            for c in (1, 2):
                moved = pltpu.roll(value, tall * wide - c, axis=0)
                xs_ref[c - 1, f] = moved.astype(jnp.bfloat16).reshape(tall, wide, mid)

    @pl.when(step < 9)
    def _():
        a, b = step // 3, step % 3
        for c in range(3):
            weights = jnp.concatenate([w_ref[3 * c + k] for k in range(3)], axis=1)
            for p in range(frames // pair):
                where = (pl.ds(a + pair * p, pair), pl.ds(b, inner))
                left = x_ref[where] if c == 0 else xs_ref[(c - 1,) + where]
                size = pair * inner * wide
                acc_ref[p * size : (p + 1) * size] += lax.dot_general(
                    left.reshape(size, mid), weights, (((1,), (1,)), ((), ())),
                    preferred_element_type=jnp.float32,
                )

    @pl.when(step == 9)
    def _():
        up_ref[...] = jnp.zeros_like(up_ref)
        size = inner * wide

        @pl.loop(0, frames)
        def _(f):
            at = pl.ds(pl.multiple_of(f * size, size), size)
            value = acc_ref[at] + feat_ref[f].reshape(size, mid).astype(jnp.float32)
            value = jnp.where(mask_ref[...] > 0, value, 0.0)
            for c in range(3):
                moved = value if c == 0 else pltpu.roll(value, size - c, axis=0)
                mx_ref[c, f] = moved.astype(jnp.bfloat16).reshape(inner, wide, mid)

    @pl.when(step >= 9)
    def _():
        b = step - 9
        for c in range(3):
            for p in range(frames // pair):
                left = mx_ref[c, pl.ds(pair * p, pair), pl.ds(b, rows), pl.ds(0, cols)]
                size = pair * rows * cols
                up_ref[p * size : (p + 1) * size] += jnp.dot(
                    left.reshape(size, mid), u_ref[c], preferred_element_type=jnp.float32
                )

    @pl.when(step == 11)
    def _():
        @pl.loop(0, frames * rows)
        def _(q):
            f, r = q // rows, q % rows
            value = up_ref[pl.ds(pl.multiple_of(q * cols, cols), cols)]
            value = jnp.concatenate([value, jnp.zeros((cols, 128), jnp.float32)], axis=1)
            for i in range(2):
                for j in range(2):
                    k = (2 * i + j) * out_channels
                    for h in range(tmp_ref.shape[0]):
                        part = value[:, k + 128 * h : k + 128 * h + 128]
                        tmp_ref[h, pl.ds(j, cols, stride=2), :] = part
                joined = jnp.concatenate([tmp_ref[h] for h in range(tmp_ref.shape[0])], axis=1)
                out_ref[f, 2 * r + i] = joined[:, :out_channels].astype(jnp.bfloat16)


def convs(stacked, features, mask, weights, up_weight, cols):
    total, tall, wide, mid = stacked.shape
    frames, inner = total - 2, tall - 2
    rows = inner - 2
    phases = up_weight.shape[-1]
    whole = pl.BlockSpec(memory_space=pltpu.VMEM)
    flops = 2 * frames * wide * inner * 27 * mid * mid
    return pl.pallas_call(
        convs_kernel,
        grid=(12,),
        out_shape=jax.ShapeDtypeStruct((frames, 2 * rows, 2 * cols, phases // 4), jnp.bfloat16),
        in_specs=[
            whole,
            whole,
            whole,
            pl.BlockSpec((9, mid, weights.shape[2]), lambda i: (jnp.minimum(i, 8), 0, 0)),
            pl.BlockSpec((3, mid, phases), lambda i: (jnp.maximum(i - 9, 0), 0, 0)),
        ],
        out_specs=whole,
        scratch_shapes=[
            pltpu.VMEM((2, total, tall, wide, mid), jnp.bfloat16),
            pltpu.VMEM((frames * inner * wide, mid), jnp.float32),
            pltpu.VMEM((3, frames, inner, wide, mid), jnp.bfloat16),
            pltpu.VMEM((frames * rows * cols, phases), jnp.float32),
            pltpu.VMEM((-(-phases // 512), 2 * cols, 128), jnp.float32),
        ],
        compiler_params=pltpu.CompilerParams(vmem_limit_bytes=48 * 2**20),
        cost_estimate=pl.CostEstimate(flops=flops, bytes_accessed=16 * 2**20, transcendentals=0),
    )(stacked, features, mask, weights, up_weight)


def local(
    n, latent, latent_mean, latent_scale, cache_latent, input_weight,
    mid_gain, mid_cache, mid_weight, up_weight,
):
    s = lax.axis_index("section")
    t = lax.axis_index("tile")
    channels = latent_mean.shape[0]
    mid = input_weight.shape[-1]
    cw = mid_weight.shape[-1]
    lanes = 128
    _, rows, cols, _ = mid_cache.shape[1:]
    shard = mid_weight.reshape(-1, lanes, cw).transpose(0, 2, 1)
    gathered, latx, clx, mcv, mch = exchange(
        n, shard, latent[0], cache_latent[0], mid_cache[0]
    )
    width = latx.shape[-1]
    frames = 2 * latx.shape[2]
    near = latx.transpose(1, 2, 0, 3, 4).reshape(frames, 3 * rows, width)[:, rows - 3 : 2 * rows + 3]
    repeats = width // channels
    scaled = (
        near.astype(jnp.float32) * jnp.tile(latent_scale, repeats) + jnp.tile(latent_mean, repeats)
    ).astype(jnp.bfloat16)
    cached = clx.transpose(2, 0, 3, 1, 4).reshape(clx.shape[2], 3 * rows, width)
    cached = cached[:, rows - 3 : 2 * rows + 3]
    joined = jnp.concatenate([cached, scaled], axis=0)
    joined = jnp.where(inside(t * rows - 3, rows + 6, n * rows)[:, None], joined, 0)
    joined = jnp.pad(joined, ((0, 0), (0, 0), (3 * channels, 3 * channels)))
    joined = lax.dynamic_slice_in_dim(joined, s * cols * channels, (cols + 6) * channels, axis=2)
    joined = joined.reshape(joined.shape[0], rows + 6, cols + 6, channels)
    features = lax.conv_general_dilated(
        joined[None], input_weight, (1, 1, 1), [(0, 0)] * 3,
        dimension_numbers=("NDHWC", "DHWIO", "NDHWC"),
        preferred_element_type=jnp.float32,
    )[0].astype(jnp.bfloat16)
    sided = jnp.concatenate([mch[0, :, :2], mch[1], mch[2, :, :2]], axis=1)
    sided = lax.dynamic_slice_in_dim(sided, 14 * s, 2, axis=2)
    centre = jnp.concatenate([mcv[0], mid_cache[0], mcv[1]], axis=1)
    cache = jnp.concatenate([sided, centre, sided], axis=2)
    stacked = jnp.concatenate([cache, activate(features, mid_gain)], axis=0)
    row_ok = inside(t * rows - 2, rows + 4, n * rows)[:, None, None]
    col_ok = inside(s * cols - 2, cols + 4, 2 * cols)[:, None]
    stacked = jnp.where(jnp.logical_and(row_ok, col_ok), stacked, 0)
    wide = -(-(cols + 4) // 16) * 16
    stacked = jnp.pad(stacked, ((0, 0), (0, 0), (0, wide - cols - 4), (0, 0)))
    inner = jnp.pad(features[:, 1:-1, 1:], ((0, 0), (0, 0), (0, wide - cols - 3), (0, 0)))
    keep = jnp.logical_and(row_ok, col_ok)[1:-1, 1:]
    keep = jnp.pad(keep, ((0, 0), (0, wide - cols - 3), (0, 0))).astype(jnp.float32)
    out = convs(
        stacked, inner, keep.reshape(-1, 1), gathered.reshape(gathered.shape[0], mid, lanes),
        up_weight.reshape((9,) + up_weight.shape[2:]), cols,
    )
    return out[None]


def solution(mesh):
    return jax.shard_map(
        functools.partial(local, mesh.shape["tile"]),
        mesh=mesh,
        in_specs=(
            P("grp", "section", "tile", None),
            P(),
            P(),
            P("grp", None, "tile", "section"),
            P(),
            P(),
            P("grp", None, "tile", "section", None),
            P(None, None, None, None, "tile"),
            P(),
        ),
        out_specs=P("grp", None, "tile", "section", None),
        check_vma=False,
    )
```

```python
import functools

import jax
import jax.numpy as jnp
from jax import lax
from jax.experimental import pallas as pl
from jax.experimental.pallas import tpu as pltpu
from jax.sharding import PartitionSpec as P

MESH = pl.DeviceIdType.MESH
PIECES = 8
PARTS = 2


def exchange_kernel(
    n, w_ref, lat_ref, cl_ref, mc_ref,
    g_ref, latx_ref, clx_ref, mcv_ref, mch_ref,
    own_sem, hs_sem, hr_sem, zs_sem, zr_sem, ps_sem, pr_sem, ss_sem, sr_sem,
):
    s = lax.axis_index("section")
    g = lax.axis_index("grp")
    t = lax.axis_index("tile")
    gx = g + 1 - 2 * (g % 2)
    gy = g + 2 - 4 * ((g // 2) % 2)
    gd = gx + 2 - 4 * ((gx // 2) % 2)
    o = 1 - s
    chunks = w_ref.shape[0]
    per = chunks // PIECES
    span = per // PARTS
    half = span // 2
    rest = chunks - per * PIECES
    has = {-1: t > 0, 0: None, 1: t < n - 1}

    def dev(ds=0, group=None, dt=0):
        return {
            "section": o if ds else s,
            "grp": g if group is None else group,
            "tile": t + dt,
        }

    def guarded(cond, fn):
        if cond is None:
            fn()
        else:
            pl.when(cond)(fn)

    partners = [(dev(1), None), (dev(0, gx), None), (dev(0, gy), None)]
    for dt in (-1, 1):
        partners += [(dev(0, None, dt), has[dt]), (dev(1, None, dt), has[dt])]
    barrier = pltpu.get_barrier_semaphore()
    for target, cond in partners:
        guarded(
            cond,
            functools.partial(
                pl.semaphore_signal, barrier, inc=1, device_id=target, device_id_type=MESH
            ),
        )
    own = [
        pltpu.make_async_copy(w_ref, g_ref.at[t], own_sem.at[0]),
        pltpu.make_async_copy(lat_ref, latx_ref.at[1, s], own_sem.at[1]),
        pltpu.make_async_copy(cl_ref, clx_ref.at[1, s], own_sem.at[2]),
    ]
    for copy in own:
        copy.start()
    pl.semaphore_wait(barrier, 3 + 2 * (jnp.minimum(t, 1) + jnp.minimum(n - 1 - t, 1)))

    def remote(src, dst, ssem, rsem, target):
        return pltpu.make_async_remote_copy(
            src_ref=src, dst_ref=dst, send_sem=ssem, recv_sem=rsem,
            device_id=target, device_id_type=MESH,
        )

    rows, cols = mc_ref.shape[1], mc_ref.shape[2]
    edge = pl.multiple_of((cols - 16) * o, 16)
    halo = []
    for dt in (-1, 0, 1):
        first = 0 if dt < 0 else rows - 2
        for ds in (0, 1):
            if (ds, dt) == (0, 0):
                continue
            k = len(halo)
            base = 3 * k
            sems = [(hs_sem.at[base + j], hr_sem.at[base + j]) for j in range(3)]
            target = dev(ds, None, dt)
            back = len(halo)
            copies = [
                (lat_ref, latx_ref.at[1 - dt, s]),
                (cl_ref, clx_ref.at[1 - dt, s]),
            ]
            if ds == 0:
                copies.append((mc_ref.at[:, pl.ds(first, 2)], mcv_ref.at[(1 - dt) // 2]))
            elif dt == 0:
                copies.append((mc_ref.at[:, :, pl.ds(edge, 16)], mch_ref.at[1]))
            else:
                copies.append(
                    (
                        mc_ref.at[:, pl.ds(first, 2), pl.ds(edge, 16)],
                        mch_ref.at[1 - dt, :, pl.ds(0, 2)],
                    )
                )
            halo.append(
                (
                    dt,
                    ds,
                    [remote(a, b, x, y, target) for (a, b), (x, y) in zip(copies, sems)],
                )
            )

    events = []
    for i in range(n - 1):
        for d in (0, 1):
            if d == 0:
                events.append((i, d, t - 1 - i, t - 1 - i >= 0))
            else:
                events.append((i, d, t + 1 + i, t + 1 + i <= n - 1))

    def begin_of(group, q):
        return (2 * (group % 4) + s) * per + q * span

    def block(group, part, q, u):
        begin = begin_of(group, q)
        if part == 0:
            return g_ref.at[u, pl.ds(begin, half)]
        if part == 1:
            return g_ref.at[u, pl.ds(begin + half, span - half)]
        return g_ref.at[u, pl.ds(begin, span)]

    tail = pl.ds(per * PIECES, rest)

    def z_copies(i, d, q, u, first):
        e = (2 * i + d) * PARTS + q
        target = dev(0, None, 1 if d == 0 else -1)
        src = w_ref.at[pl.ds(begin_of(g, q), span)] if first else block(g, 2, q, u)
        made = [remote(src, block(g, 2, q, u), zs_sem.at[2 * e], zr_sem.at[2 * e], target)]
        if q == PARTS - 1 and rest:
            src = w_ref.at[tail] if first else g_ref.at[u, tail]
            k = 2 * e + 1
            made.append(remote(src, g_ref.at[u, tail], zs_sem.at[k], zr_sem.at[k], target))
        return made

    def d_copies(e, q, u):
        def one(k, group, part, to):
            b = block(group, part, q, u)
            return remote(b, b, ps_sem.at[6 * e + k], pr_sem.at[6 * e + k], dev(0, to))

        first = [one(0, g, 0, gx), one(1, g, 1, gy)]
        second = [one(2, g, 0, gy), one(3, gx, 0, gy), one(4, g, 1, gx), one(5, gy, 1, gx)]
        return first, second

    def s_copies(e, q, u):
        plan = [(g, 2), (gx, 0), (gy, 1), (gy, 0), (gd, 0), (gx, 1), (gd, 1)]
        made = []
        for k, (group, part) in enumerate(plan):
            b = block(group, part, q, u)
            made.append(remote(b, b, ss_sem.at[7 * e + k], sr_sem.at[7 * e + k], dev(1)))
        return made

    def begin_z(i, d, q, u, valid, first):
        dt = 1 if d == 0 else -1

        def go():
            for copy in z_copies(i, d, q, u, first):
                copy.start()

        pl.when(jnp.logical_and(valid, has[dt]))(go)

    def end_z(i, d, q, u, valid):
        dt = 1 if d == 0 else -1

        def go():
            for copy in z_copies(i, d, q, u, i == 0):
                copy.wait_send()

        pl.when(jnp.logical_and(valid, has[dt]))(go)

    for q in range(PARTS):
        begin_z(0, 0, q, t, t >= 0, True)
        begin_z(0, 1, q, t, t >= 0, True)
    for dt, ds, copies in halo:
        def go(copies=copies):
            for copy in copies:
                copy.start()
        guarded(has[dt], go)

    def arrive(i, d, q, u):
        for copy in z_copies(i, d, q, u, False):
            copy.wait_recv()

    def stage_a(i, d, q, u, valid):
        e = (2 * i + d) * PARTS + q

        def go():
            arrive(i, d, q, u)
            if i + 1 < n - 1:
                begin_z(i + 1, d, q, u, valid, False)
            for copy in d_copies(e, q, u)[0]:
                copy.start()
            s_copies(e, q, u)[0].start()

        pl.when(valid)(go)

    def stage_b(i, d, q, u, valid):
        e = (2 * i + d) * PARTS + q

        def go():
            first, second = d_copies(e, q, u)
            sib = s_copies(e, q, u)
            first[0].wait_recv()
            second[0].start()
            second[1].start()
            sib[1].start()
            first[1].wait_recv()
            second[2].start()
            second[3].start()
            sib[2].start()

        pl.when(valid)(go)

    def stage_c(i, d, q, u, valid):
        e = (2 * i + d) * PARTS + q

        def go():
            _, second = d_copies(e, q, u)
            sib = s_copies(e, q, u)
            for k in range(4):
                second[k].wait_recv()
                sib[3 + k].start()

        pl.when(valid)(go)

    for slot in range((n - 1) * PARTS + 2):
        for stage, lag in ((stage_a, 0), (stage_b, 1), (stage_c, 2)):
            i, q = (slot - lag) // PARTS, (slot - lag) % PARTS
            if 0 <= i < n - 1:
                for _, d, u, valid in events[2 * i : 2 * i + 2]:
                    stage(i, d, q, u, valid)

    for copy in own:
        copy.wait()
    for dt, ds, copies in halo:
        guarded(has[dt], lambda copies=copies: [c.wait_send() for c in copies] and None)
    order = {(dt, ds): copies for dt, ds, copies in halo}
    for (dt, ds), copies in order.items():
        guarded(has[-dt], lambda copies=copies: [c.wait_recv() for c in copies] and None)
    for i, d, u, valid in events:
        for q in range(PARTS):
            e = (2 * i + d) * PARTS + q

            def finish(e=e, q=q, u=u):
                first, second = d_copies(e, q, u)
                for copy in first + second:
                    copy.wait_send()
                for copy in s_copies(e, q, u):
                    copy.wait()

            pl.when(valid)(finish)
            sent = t - i if d == 0 else t + i
            end_z(i, d, q, sent, sent >= 0 if d == 0 else sent <= n - 1)


def exchange(n, weights, latent, cache_latent, mid_cache):
    frames, rows, cols, channels = mid_cache.shape
    dt = weights.dtype
    shape = jax.ShapeDtypeStruct
    events = 2 * (n - 1) * PARTS
    dma = lambda k: pltpu.SemaphoreType.DMA((k,))
    return pl.pallas_call(
        functools.partial(exchange_kernel, n),
        out_shape=(
            shape((n,) + weights.shape, dt),
            shape((3, 2) + latent.shape, dt),
            shape((3, 2) + cache_latent.shape, dt),
            shape((2, frames, 2, cols, channels), dt),
            shape((3, frames, rows, 16, channels), dt),
        ),
        in_specs=[pl.BlockSpec(memory_space=pl.ANY)] * 4,
        out_specs=[pl.BlockSpec(memory_space=pl.ANY)] * 5,
        scratch_shapes=[
            dma(3), dma(15), dma(15), dma(2 * events), dma(2 * events),
            dma(6 * events), dma(6 * events), dma(7 * events), dma(7 * events),
        ],
        compiler_params=pltpu.CompilerParams(collective_id=0, has_side_effects=True),
    )(weights, latent, cache_latent, mid_cache)


def activate(values, gain_vector):
    floats = values.astype(jnp.float32)
    inverse_rms = lax.rsqrt(jnp.mean(floats * floats, axis=-1, keepdims=True) + 1e-06)
    return jax.nn.silu(floats * inverse_rms * gain_vector).astype(jnp.bfloat16)


def inside(start, count, limit):
    index = start + jnp.arange(count)
    return jnp.logical_and(index >= 0, index < limit)


def convs_kernel(
    x_ref, feat_ref, mask_ref, w_ref, u_ref, out_ref, xs_ref, acc_ref, mx_ref, up_ref, tmp_ref
):
    step = pl.program_id(0)
    total, tall, wide, mid = x_ref.shape
    frames, inner = total - 2, tall - 2
    rows = inner - 2
    cols = out_ref.shape[2] // 2
    out_channels = out_ref.shape[3]

    @pl.when(step == 0)
    def _():
        acc_ref[...] = jnp.zeros_like(acc_ref)

        @pl.loop(0, total)
        def _(f):
            value = x_ref[f].reshape(tall * wide, mid).astype(jnp.float32)
            for c in (1, 2):
                moved = pltpu.roll(value, tall * wide - c, axis=0)
                xs_ref[c - 1, f] = moved.astype(jnp.bfloat16).reshape(tall, wide, mid)

    @pl.when(step < 9)
    def _():
        a, b = step // 3, step % 3
        where = (pl.ds(a, frames), pl.ds(b, inner))
        size = frames * inner * wide
        left = [x_ref[where]] + [xs_ref[(c,) + where] for c in range(2)]
        left = jnp.concatenate([v.reshape(size, mid) for v in left], axis=1)
        weights = [
            jnp.concatenate([w_ref[u, c] for u in range(w_ref.shape[0])], axis=0)
            for c in range(3)
        ]
        acc_ref[...] += lax.dot_general(
            left, jnp.concatenate(weights, axis=1), (((1,), (1,)), ((), ())),
            preferred_element_type=jnp.float32,
        )

    @pl.when(step == 9)
    def _():
        up_ref[...] = jnp.zeros_like(up_ref)
        size = inner * wide

        @pl.loop(0, frames)
        def _(f):
            at = pl.ds(pl.multiple_of(f * size, size), size)
            value = acc_ref[at] + feat_ref[f].reshape(size, mid).astype(jnp.float32)
            value = jnp.where(mask_ref[...] > 0, value, 0.0)
            for c in range(3):
                moved = value if c == 0 else pltpu.roll(value, size - c, axis=0)
                mx_ref[c, f] = moved.astype(jnp.bfloat16).reshape(inner, wide, mid)

    @pl.when(step >= 9)
    def _():
        b = step - 9
        size = frames * rows * cols
        left = [mx_ref[c, :, pl.ds(b, rows), pl.ds(0, cols)] for c in range(3)]
        left = jnp.concatenate([v.reshape(size, mid) for v in left], axis=1)
        up_ref[...] += jnp.dot(
            left, u_ref[...].reshape(3 * mid, u_ref.shape[2]), preferred_element_type=jnp.float32
        )

    @pl.when(step == 11)
    def _():
        @pl.loop(0, frames * rows)
        def _(q):
            f, r = q // rows, q % rows
            value = up_ref[pl.ds(pl.multiple_of(q * cols, cols), cols)]
            value = jnp.concatenate([value, jnp.zeros((cols, 128), jnp.float32)], axis=1)
            for i in range(2):
                for j in range(2):
                    k = (2 * i + j) * out_channels
                    for h in range(tmp_ref.shape[0]):
                        part = value[:, k + 128 * h : k + 128 * h + 128]
                        tmp_ref[h, pl.ds(j, cols, stride=2), :] = part
                joined = jnp.concatenate([tmp_ref[h] for h in range(tmp_ref.shape[0])], axis=1)
                out_ref[f, 2 * r + i] = joined[:, :out_channels].astype(jnp.bfloat16)


def convs(stacked, features, mask, weights, up_weight, cols):
    total, tall, wide, mid = stacked.shape
    frames, inner = total - 2, tall - 2
    rows = inner - 2
    phases = up_weight.shape[-1]
    whole = pl.BlockSpec(memory_space=pltpu.VMEM)
    flops = 2 * frames * wide * inner * 27 * mid * mid
    return pl.pallas_call(
        convs_kernel,
        grid=(12,),
        out_shape=jax.ShapeDtypeStruct((frames, 2 * rows, 2 * cols, phases // 4), jnp.bfloat16),
        in_specs=[
            whole,
            whole,
            whole,
            pl.BlockSpec(
                (weights.shape[0], 3) + weights.shape[2:],
                lambda i: (0, jnp.minimum(i, 8), 0, 0),
            ),
            pl.BlockSpec((3, mid, phases), lambda i: (jnp.maximum(i - 9, 0), 0, 0)),
        ],
        out_specs=whole,
        scratch_shapes=[
            pltpu.VMEM((2, total, tall, wide, mid), jnp.bfloat16),
            pltpu.VMEM((frames * inner * wide, mid), jnp.float32),
            pltpu.VMEM((3, frames, inner, wide, mid), jnp.bfloat16),
            pltpu.VMEM((frames * rows * cols, phases), jnp.float32),
            pltpu.VMEM((-(-phases // 512), 2 * cols, 128), jnp.float32),
        ],
        compiler_params=pltpu.CompilerParams(vmem_limit_bytes=48 * 2**20),
        cost_estimate=pl.CostEstimate(flops=flops, bytes_accessed=16 * 2**20, transcendentals=0),
    )(stacked, features, mask, weights, up_weight)


def local(
    n, latent, latent_mean, latent_scale, cache_latent, input_weight,
    mid_gain, mid_cache, mid_weight, up_weight,
):
    s = lax.axis_index("section")
    t = lax.axis_index("tile")
    channels = latent_mean.shape[0]
    mid = input_weight.shape[-1]
    cw = mid_weight.shape[-1]
    _, rows, cols, _ = mid_cache.shape[1:]
    shard = mid_weight.transpose(0, 1, 2, 4, 3).reshape(-1, 16 if cw % 16 == 0 else 8, mid)
    gathered, latx, clx, mcv, mch = exchange(
        n, shard, latent[0], cache_latent[0], mid_cache[0]
    )
    width = latx.shape[-1]
    frames = 2 * latx.shape[2]
    near = latx.transpose(1, 2, 0, 3, 4).reshape(frames, 3 * rows, width)[:, rows - 3 : 2 * rows + 3]
    repeats = width // channels
    scaled = (
        near.astype(jnp.float32) * jnp.tile(latent_scale, repeats) + jnp.tile(latent_mean, repeats)
    ).astype(jnp.bfloat16)
    cached = clx.transpose(2, 0, 3, 1, 4).reshape(clx.shape[2], 3 * rows, width)
    cached = cached[:, rows - 3 : 2 * rows + 3]
    joined = jnp.concatenate([cached, scaled], axis=0)
    joined = jnp.where(inside(t * rows - 3, rows + 6, n * rows)[:, None], joined, 0)
    joined = jnp.pad(joined, ((0, 0), (0, 0), (3 * channels, 3 * channels)))
    joined = lax.dynamic_slice_in_dim(joined, s * cols * channels, (cols + 6) * channels, axis=2)
    joined = joined.reshape(joined.shape[0], rows + 6, cols + 6, channels)
    features = lax.conv_general_dilated(
        joined[None], input_weight, (1, 1, 1), [(0, 0)] * 3,
        dimension_numbers=("NDHWC", "DHWIO", "NDHWC"),
        preferred_element_type=jnp.float32,
    )[0].astype(jnp.bfloat16)
    sided = jnp.concatenate([mch[0, :, :2], mch[1], mch[2, :, :2]], axis=1)
    sided = lax.dynamic_slice_in_dim(sided, 14 * s, 2, axis=2)
    centre = jnp.concatenate([mcv[0], mid_cache[0], mcv[1]], axis=1)
    cache = jnp.concatenate([sided, centre, sided], axis=2)
    stacked = jnp.concatenate([cache, activate(features, mid_gain)], axis=0)
    row_ok = inside(t * rows - 2, rows + 4, n * rows)[:, None, None]
    col_ok = inside(s * cols - 2, cols + 4, 2 * cols)[:, None]
    stacked = jnp.where(jnp.logical_and(row_ok, col_ok), stacked, 0)
    wide = -(-(cols + 4) // 16) * 16
    stacked = jnp.pad(stacked, ((0, 0), (0, 0), (0, wide - cols - 4), (0, 0)))
    inner = jnp.pad(features[:, 1:-1, 1:], ((0, 0), (0, 0), (0, wide - cols - 3), (0, 0)))
    keep = jnp.logical_and(row_ok, col_ok)[1:-1, 1:]
    keep = jnp.pad(keep, ((0, 0), (0, wide - cols - 3), (0, 0))).astype(jnp.float32)
    out = convs(
        stacked, inner, keep.reshape(-1, 1), gathered.reshape(n, 27, cw, mid),
        up_weight.reshape((9,) + up_weight.shape[2:]), cols,
    )
    return out[None]


def solution(mesh):
    return jax.shard_map(
        functools.partial(local, mesh.shape["tile"]),
        mesh=mesh,
        in_specs=(
            P("grp", "section", "tile", None),
            P(),
            P(),
            P("grp", None, "tile", "section"),
            P(),
            P(),
            P("grp", None, "tile", "section", None),
            P(None, None, None, None, "tile"),
            P(),
        ),
        out_specs=P("grp", None, "tile", "section", None),
        check_vma=False,
    )
```

```python
import functools

import jax
import jax.numpy as jnp
from jax import lax
from jax.experimental import pallas as pl
from jax.experimental.pallas import tpu as pltpu
from jax.sharding import PartitionSpec as P

MESH = pl.DeviceIdType.MESH
PIECES = 8
PARTS = 2


def exchange_kernel(
    n, w_ref, lat_ref, cl_ref, mc_ref,
    g_ref, latx_ref, clx_ref, mcv_ref, mch_ref,
    own_sem, hs_sem, hr_sem, zs_sem, zr_sem, ps_sem, pr_sem, ss_sem, sr_sem,
):
    s = lax.axis_index("section")
    g = lax.axis_index("grp")
    t = lax.axis_index("tile")
    gx = g + 1 - 2 * (g % 2)
    gy = g + 2 - 4 * ((g // 2) % 2)
    gd = gx + 2 - 4 * ((gx // 2) % 2)
    o = 1 - s
    chunks = w_ref.shape[0]
    per = chunks // PIECES
    span = per // PARTS
    half = span // 2
    rest = chunks - per * PIECES
    has = {-1: t > 0, 0: None, 1: t < n - 1}

    def dev(ds=0, group=None, dt=0):
        return {
            "section": o if ds else s,
            "grp": g if group is None else group,
            "tile": t + dt,
        }

    def guarded(cond, fn):
        if cond is None:
            fn()
        else:
            pl.when(cond)(fn)

    partners = [(dev(1), None), (dev(0, gx), None), (dev(0, gy), None)]
    for dt in (-1, 1):
        partners += [(dev(0, None, dt), has[dt]), (dev(1, None, dt), has[dt])]
    barrier = pltpu.get_barrier_semaphore()
    for target, cond in partners:
        guarded(
            cond,
            functools.partial(
                pl.semaphore_signal, barrier, inc=1, device_id=target, device_id_type=MESH
            ),
        )
    own = [
        pltpu.make_async_copy(w_ref, g_ref.at[t], own_sem.at[0]),
        pltpu.make_async_copy(lat_ref, latx_ref.at[1, s], own_sem.at[1]),
        pltpu.make_async_copy(cl_ref, clx_ref.at[1, s], own_sem.at[2]),
    ]
    for copy in own:
        copy.start()
    pl.semaphore_wait(barrier, 3 + 2 * (jnp.minimum(t, 1) + jnp.minimum(n - 1 - t, 1)))

    def remote(src, dst, ssem, rsem, target):
        return pltpu.make_async_remote_copy(
            src_ref=src, dst_ref=dst, send_sem=ssem, recv_sem=rsem,
            device_id=target, device_id_type=MESH,
        )

    rows, cols = mc_ref.shape[1], mc_ref.shape[2]
    edge = pl.multiple_of((cols - 16) * o, 16)
    halo = []
    for dt in (-1, 0, 1):
        first = 0 if dt < 0 else rows - 2
        for ds in (0, 1):
            if (ds, dt) == (0, 0):
                continue
            k = len(halo)
            base = 3 * k
            sems = [(hs_sem.at[base + j], hr_sem.at[base + j]) for j in range(3)]
            target = dev(ds, None, dt)
            back = len(halo)
            copies = [
                (lat_ref, latx_ref.at[1 - dt, s]),
                (cl_ref, clx_ref.at[1 - dt, s]),
            ]
            if ds == 0:
                copies.append((mc_ref.at[:, pl.ds(first, 2)], mcv_ref.at[(1 - dt) // 2]))
            elif dt == 0:
                copies.append((mc_ref.at[:, :, pl.ds(edge, 16)], mch_ref.at[1]))
            else:
                copies.append(
                    (
                        mc_ref.at[:, pl.ds(first, 2), pl.ds(edge, 16)],
                        mch_ref.at[1 - dt, :, pl.ds(0, 2)],
                    )
                )
            halo.append(
                (
                    dt,
                    ds,
                    [remote(a, b, x, y, target) for (a, b), (x, y) in zip(copies, sems)],
                )
            )

    events = []
    for i in range(n - 1):
        for d in (0, 1):
            if d == 0:
                events.append((i, d, t - 1 - i, t - 1 - i >= 0))
            else:
                events.append((i, d, t + 1 + i, t + 1 + i <= n - 1))

    def begin_of(group, q):
        return (2 * (group % 4) + s) * per + q * span

    def block(group, part, q, u):
        begin = begin_of(group, q)
        if part == 0:
            return g_ref.at[u, pl.ds(begin, half)]
        if part == 1:
            return g_ref.at[u, pl.ds(begin + half, span - half)]
        return g_ref.at[u, pl.ds(begin, span)]

    tail = pl.ds(per * PIECES, rest)

    def z_copies(i, d, q, u, first):
        e = (2 * i + d) * PARTS + q
        target = dev(0, None, 1 if d == 0 else -1)
        src = w_ref.at[pl.ds(begin_of(g, q), span)] if first else block(g, 2, q, u)
        made = [remote(src, block(g, 2, q, u), zs_sem.at[2 * e], zr_sem.at[2 * e], target)]
        if q == PARTS - 1 and rest:
            src = w_ref.at[tail] if first else g_ref.at[u, tail]
            k = 2 * e + 1
            made.append(remote(src, g_ref.at[u, tail], zs_sem.at[k], zr_sem.at[k], target))
        return made

    def d_copies(e, q, u):
        def one(k, group, part, to):
            b = block(group, part, q, u)
            return remote(b, b, ps_sem.at[6 * e + k], pr_sem.at[6 * e + k], dev(0, to))

        first = [one(0, g, 0, gx), one(1, g, 1, gy)]
        second = [one(2, g, 0, gy), one(3, gx, 0, gy), one(4, g, 1, gx), one(5, gy, 1, gx)]
        return first, second

    def s_copies(e, q, u):
        plan = [(g, 2), (gx, 0), (gy, 1), (gy, 0), (gd, 0), (gx, 1), (gd, 1)]
        made = []
        for k, (group, part) in enumerate(plan):
            b = block(group, part, q, u)
            made.append(remote(b, b, ss_sem.at[7 * e + k], sr_sem.at[7 * e + k], dev(1)))
        return made

    def begin_z(i, d, q, u, valid, first):
        dt = 1 if d == 0 else -1

        def go():
            for copy in z_copies(i, d, q, u, first):
                copy.start()

        pl.when(jnp.logical_and(valid, has[dt]))(go)

    def end_z(i, d, q, u, valid):
        dt = 1 if d == 0 else -1

        def go():
            for copy in z_copies(i, d, q, u, i == 0):
                copy.wait_send()

        pl.when(jnp.logical_and(valid, has[dt]))(go)

    for q in range(PARTS):
        begin_z(0, 0, q, t, t >= 0, True)
        begin_z(0, 1, q, t, t >= 0, True)
    for dt, ds, copies in halo:
        def go(copies=copies):
            for copy in copies:
                copy.start()
        guarded(has[dt], go)

    def arrive(i, d, q, u):
        for copy in z_copies(i, d, q, u, False):
            copy.wait_recv()

    def stage_a(i, d, q, u, valid):
        e = (2 * i + d) * PARTS + q

        def go():
            arrive(i, d, q, u)
            if i + 1 < n - 1:
                begin_z(i + 1, d, q, u, valid, False)
            for copy in d_copies(e, q, u)[0]:
                copy.start()
            s_copies(e, q, u)[0].start()

        pl.when(valid)(go)

    def stage_b(i, d, q, u, valid):
        e = (2 * i + d) * PARTS + q

        def go():
            first, second = d_copies(e, q, u)
            sib = s_copies(e, q, u)
            first[0].wait_recv()
            second[0].start()
            second[1].start()
            sib[1].start()
            first[1].wait_recv()
            second[2].start()
            second[3].start()
            sib[2].start()

        pl.when(valid)(go)

    def stage_c(i, d, q, u, valid):
        e = (2 * i + d) * PARTS + q

        def go():
            _, second = d_copies(e, q, u)
            sib = s_copies(e, q, u)
            for k in range(4):
                second[k].wait_recv()
                sib[3 + k].start()

        pl.when(valid)(go)

    for slot in range((n - 1) * PARTS + 2):
        for stage, lag in ((stage_a, 0), (stage_b, 1), (stage_c, 2)):
            i, q = (slot - lag) // PARTS, (slot - lag) % PARTS
            if 0 <= i < n - 1:
                for _, d, u, valid in events[2 * i : 2 * i + 2]:
                    stage(i, d, q, u, valid)

    for copy in own:
        copy.wait()
    for dt, ds, copies in halo:
        guarded(has[dt], lambda copies=copies: [c.wait_send() for c in copies] and None)
    order = {(dt, ds): copies for dt, ds, copies in halo}
    for (dt, ds), copies in order.items():
        guarded(has[-dt], lambda copies=copies: [c.wait_recv() for c in copies] and None)
    for i, d, u, valid in events:
        for q in range(PARTS):
            e = (2 * i + d) * PARTS + q

            def finish(e=e, q=q, u=u):
                first, second = d_copies(e, q, u)
                for copy in first + second:
                    copy.wait_send()
                for copy in s_copies(e, q, u):
                    copy.wait()

            pl.when(valid)(finish)
            sent = t - i if d == 0 else t + i
            end_z(i, d, q, sent, sent >= 0 if d == 0 else sent <= n - 1)


def exchange(n, weights, latent, cache_latent, mid_cache):
    frames, rows, cols, channels = mid_cache.shape
    dt = weights.dtype
    shape = jax.ShapeDtypeStruct
    events = 2 * (n - 1) * PARTS
    dma = lambda k: pltpu.SemaphoreType.DMA((k,))
    return pl.pallas_call(
        functools.partial(exchange_kernel, n),
        out_shape=(
            shape((n,) + weights.shape, dt),
            shape((3, 2) + latent.shape, dt),
            shape((3, 2) + cache_latent.shape, dt),
            shape((2, frames, 2, cols, channels), dt),
            shape((3, frames, rows, 16, channels), dt),
        ),
        in_specs=[pl.BlockSpec(memory_space=pl.ANY)] * 4,
        out_specs=[pl.BlockSpec(memory_space=pl.ANY)] * 5,
        scratch_shapes=[
            dma(3), dma(15), dma(15), dma(2 * events), dma(2 * events),
            dma(6 * events), dma(6 * events), dma(7 * events), dma(7 * events),
        ],
        compiler_params=pltpu.CompilerParams(collective_id=0, has_side_effects=True),
    )(weights, latent, cache_latent, mid_cache)


def inside(start, count, limit):
    index = start + jnp.arange(count)
    return jnp.logical_and(index >= 0, index < limit)


def convs_kernel(
    beside_ref, taps_ref, gain_ref, cache_ref, region_ref, mask_ref, w_ref, u_ref, out_ref,
    x_ref, feat_ref, xs_ref, acc_ref, mx_ref, up_ref, tmp_ref,
):
    step = pl.program_id(0)
    total, tall, wide, mid = x_ref.shape
    frames, inner = total - 2, tall - 2
    rows = inner - 2
    cols = out_ref.shape[2] // 2
    out_channels = out_ref.shape[3]

    @pl.when(step == 0)
    def _():
        acc_ref[...] = jnp.zeros_like(acc_ref)
        x_ref[0 : total - frames] = cache_ref[...]
        size = tall * wide

        @pl.loop(0, frames)
        def _(f):
            value = jnp.zeros((size, mid), jnp.float32)
            for a in range(3):
                for b in range(3):
                    left = beside_ref[f + a, b : b + tall].reshape(size, beside_ref.shape[3])
                    value += jnp.dot(
                        left, taps_ref[3 * a + b], preferred_element_type=jnp.float32
                    )
            value = value.astype(jnp.bfloat16).astype(jnp.float32)
            moved = pltpu.roll(value, size - 1, axis=0).reshape(tall, wide, mid)
            feat_ref[f] = moved[1:-1].astype(jnp.bfloat16)
            power = jnp.mean(value * value, axis=-1, keepdims=True)
            value = value * lax.rsqrt(power + 1e-06) * gain_ref[...]
            value = jnp.where(region_ref[...] > 0, value / (1.0 + jnp.exp(-value)), 0.0)
            x_ref[total - frames + f] = value.astype(jnp.bfloat16).reshape(tall, wide, mid)

        @pl.loop(0, total)
        def _(f):
            value = x_ref[f].reshape(tall * wide, mid).astype(jnp.float32)
            for c in (1, 2):
                moved = pltpu.roll(value, tall * wide - c, axis=0)
                xs_ref[c - 1, f] = moved.astype(jnp.bfloat16).reshape(tall, wide, mid)

    @pl.when(step < 9)
    def _():
        a, b = step // 3, step % 3
        where = (pl.ds(a, frames), pl.ds(b, inner))
        size = frames * inner * wide
        left = [x_ref[where]] + [xs_ref[(c,) + where] for c in range(2)]
        left = jnp.concatenate([v.reshape(size, mid) for v in left], axis=1)
        weights = [
            jnp.concatenate([w_ref[u, c] for u in range(w_ref.shape[0])], axis=0)
            for c in range(3)
        ]
        acc_ref[...] += lax.dot_general(
            left, jnp.concatenate(weights, axis=1), (((1,), (1,)), ((), ())),
            preferred_element_type=jnp.float32,
        )

    @pl.when(step == 9)
    def _():
        up_ref[...] = jnp.zeros_like(up_ref)
        size = inner * wide

        @pl.loop(0, frames)
        def _(f):
            at = pl.ds(pl.multiple_of(f * size, size), size)
            value = acc_ref[at] + feat_ref[f].reshape(size, mid).astype(jnp.float32)
            value = jnp.where(mask_ref[...] > 0, value, 0.0)
            for c in range(3):
                moved = value if c == 0 else pltpu.roll(value, size - c, axis=0)
                mx_ref[c, f] = moved.astype(jnp.bfloat16).reshape(inner, wide, mid)

    @pl.when(step >= 9)
    def _():
        b = step - 9
        size = frames * rows * cols
        left = [mx_ref[c, :, pl.ds(b, rows), pl.ds(0, cols)] for c in range(3)]
        left = jnp.concatenate([v.reshape(size, mid) for v in left], axis=1)
        up_ref[...] += jnp.dot(
            left, u_ref[...].reshape(3 * mid, u_ref.shape[2]), preferred_element_type=jnp.float32
        )

    @pl.when(step == 11)
    def _():
        @pl.loop(0, frames * rows)
        def _(q):
            f, r = q // rows, q % rows
            value = up_ref[pl.ds(pl.multiple_of(q * cols, cols), cols)]
            value = jnp.concatenate([value, jnp.zeros((cols, 128), jnp.float32)], axis=1)
            for i in range(2):
                for j in range(2):
                    k = (2 * i + j) * out_channels
                    for h in range(tmp_ref.shape[0]):
                        part = value[:, k + 128 * h : k + 128 * h + 128]
                        tmp_ref[h, pl.ds(j, cols, stride=2), :] = part
                joined = jnp.concatenate([tmp_ref[h] for h in range(tmp_ref.shape[0])], axis=1)
                out_ref[f, 2 * r + i] = joined[:, :out_channels].astype(jnp.bfloat16)


def convs(beside, taps, gain, cache, region, mask, weights, up_weight, cols):
    total = beside.shape[0]
    tall, wide, mid = cache.shape[1:]
    frames, inner = total - 2, tall - 2
    rows = inner - 2
    phases = up_weight.shape[-1]
    whole = pl.BlockSpec(memory_space=pltpu.VMEM)
    flops = 2 * frames * wide * inner * 27 * mid * mid
    return pl.pallas_call(
        convs_kernel,
        grid=(12,),
        out_shape=jax.ShapeDtypeStruct((frames, 2 * rows, 2 * cols, phases // 4), jnp.bfloat16),
        in_specs=[
            whole,
            whole,
            whole,
            whole,
            whole,
            whole,
            pl.BlockSpec(
                (weights.shape[0], 3) + weights.shape[2:],
                lambda i: (0, jnp.minimum(i, 8), 0, 0),
            ),
            pl.BlockSpec((3, mid, phases), lambda i: (jnp.maximum(i - 9, 0), 0, 0)),
        ],
        out_specs=whole,
        scratch_shapes=[
            pltpu.VMEM((total, tall, wide, mid), jnp.bfloat16),
            pltpu.VMEM((frames, inner, wide, mid), jnp.bfloat16),
            pltpu.VMEM((2, total, tall, wide, mid), jnp.bfloat16),
            pltpu.VMEM((frames * inner * wide, mid), jnp.float32),
            pltpu.VMEM((3, frames, inner, wide, mid), jnp.bfloat16),
            pltpu.VMEM((frames * rows * cols, phases), jnp.float32),
            pltpu.VMEM((-(-phases // 512), 2 * cols, 128), jnp.float32),
        ],
        compiler_params=pltpu.CompilerParams(vmem_limit_bytes=48 * 2**20),
        cost_estimate=pl.CostEstimate(flops=flops, bytes_accessed=16 * 2**20, transcendentals=0),
    )(beside, taps, gain, cache, region, mask, weights, up_weight)


def local(
    n, latent, latent_mean, latent_scale, cache_latent, input_weight,
    mid_gain, mid_cache, mid_weight, up_weight,
):
    s = lax.axis_index("section")
    t = lax.axis_index("tile")
    channels = latent_mean.shape[0]
    mid = input_weight.shape[-1]
    cw = mid_weight.shape[-1]
    _, rows, cols, _ = mid_cache.shape[1:]
    shard = mid_weight.transpose(0, 1, 2, 4, 3).reshape(-1, 16 if cw % 16 == 0 else 8, mid)
    gathered, latx, clx, mcv, mch = exchange(
        n, shard, latent[0], cache_latent[0], mid_cache[0]
    )
    width = latx.shape[-1]
    frames = 2 * latx.shape[2]
    near = latx.transpose(1, 2, 0, 3, 4).reshape(frames, 3 * rows, width)[:, rows - 3 : 2 * rows + 3]
    repeats = width // channels
    scaled = (
        near.astype(jnp.float32) * jnp.tile(latent_scale, repeats) + jnp.tile(latent_mean, repeats)
    ).astype(jnp.bfloat16)
    cached = clx.transpose(2, 0, 3, 1, 4).reshape(clx.shape[2], 3 * rows, width)
    cached = cached[:, rows - 3 : 2 * rows + 3]
    joined = jnp.concatenate([cached, scaled], axis=0)
    joined = jnp.where(inside(t * rows - 3, rows + 6, n * rows)[:, None], joined, 0)
    joined = jnp.pad(joined, ((0, 0), (0, 0), (3 * channels, 3 * channels)))
    joined = lax.dynamic_slice_in_dim(joined, s * cols * channels, (cols + 6) * channels, axis=2)
    joined = joined.reshape(joined.shape[0], rows + 6, cols + 6, channels)
    wide = -(-(cols + 4) // 16) * 16
    extra = wide - cols - 4
    beside = jnp.concatenate([joined[:, :, c : c + cols + 4] for c in range(3)], axis=-1)
    beside = jnp.pad(beside, ((0, 0), (0, 0), (0, extra), (0, 0)))
    sided = jnp.concatenate([mch[0, :, :2], mch[1], mch[2, :, :2]], axis=1)
    sided = lax.dynamic_slice_in_dim(sided, 14 * s, 2, axis=2)
    centre = jnp.concatenate([mcv[0], mid_cache[0], mcv[1]], axis=1)
    cache = jnp.concatenate([sided, centre, sided], axis=2)
    row_ok = inside(t * rows - 2, rows + 4, n * rows)[:, None, None]
    col_ok = inside(s * cols - 2, cols + 4, 2 * cols)[:, None]
    region = jnp.logical_and(row_ok, col_ok)
    cache = jnp.pad(jnp.where(region, cache, 0), ((0, 0), (0, 0), (0, extra), (0, 0)))
    keep = jnp.pad(region[1:-1, 1:], ((0, 0), (0, extra + 1), (0, 0))).astype(jnp.float32)
    region = jnp.pad(region, ((0, 0), (0, extra), (0, 0))).astype(jnp.float32)
    out = convs(
        beside, input_weight.reshape(9, 3 * channels, mid), mid_gain[None], cache,
        region.reshape(-1, 1), keep.reshape(-1, 1), gathered.reshape(n, 27, cw, mid),
        up_weight.reshape((9,) + up_weight.shape[2:]), cols,
    )
    return out[None]


def solution(mesh):
    return jax.shard_map(
        functools.partial(local, mesh.shape["tile"]),
        mesh=mesh,
        in_specs=(
            P("grp", "section", "tile", None),
            P(),
            P(),
            P("grp", None, "tile", "section"),
            P(),
            P(),
            P("grp", None, "tile", "section", None),
            P(None, None, None, None, "tile"),
            P(),
        ),
        out_specs=P("grp", None, "tile", "section", None),
        check_vma=False,
    )
```

```python
import functools

import jax
import jax.numpy as jnp
from jax import lax
from jax.experimental import pallas as pl
from jax.experimental.pallas import tpu as pltpu
from jax.sharding import PartitionSpec as P

MESH = pl.DeviceIdType.MESH
PIECES = 8
PARTS = 1


def exchange_kernel(
    n, w_ref, lat_ref, cl_ref, mc_ref,
    g_ref, latx_ref, clx_ref, mcv_ref, mch_ref,
    own_sem, hs_sem, hr_sem, zs_sem, zr_sem, ps_sem, pr_sem, ss_sem, sr_sem,
):
    s = lax.axis_index("section")
    g = lax.axis_index("grp")
    t = lax.axis_index("tile")
    gx = g + 1 - 2 * (g % 2)
    gy = g + 2 - 4 * ((g // 2) % 2)
    gd = gx + 2 - 4 * ((gx // 2) % 2)
    o = 1 - s
    chunks = w_ref.shape[0]
    per = chunks // PIECES
    span = per // PARTS
    half = span // 2
    rest = chunks - per * PIECES
    has = {-1: t > 0, 0: None, 1: t < n - 1}

    def dev(ds=0, group=None, dt=0):
        return {
            "section": o if ds else s,
            "grp": g if group is None else group,
            "tile": t + dt,
        }

    def guarded(cond, fn):
        if cond is None:
            fn()
        else:
            pl.when(cond)(fn)

    partners = [(dev(1), None), (dev(0, gx), None), (dev(0, gy), None)]
    for dt in (-1, 1):
        partners += [(dev(0, None, dt), has[dt]), (dev(1, None, dt), has[dt])]
    barrier = pltpu.get_barrier_semaphore()
    for target, cond in partners:
        guarded(
            cond,
            functools.partial(
                pl.semaphore_signal, barrier, inc=1, device_id=target, device_id_type=MESH
            ),
        )
    own = [
        pltpu.make_async_copy(w_ref, g_ref.at[t], own_sem.at[0]),
        pltpu.make_async_copy(lat_ref, latx_ref.at[1, s], own_sem.at[1]),
        pltpu.make_async_copy(cl_ref, clx_ref.at[1, s], own_sem.at[2]),
    ]
    for copy in own:
        copy.start()
    pl.semaphore_wait(barrier, 3 + 2 * (jnp.minimum(t, 1) + jnp.minimum(n - 1 - t, 1)))

    def remote(src, dst, ssem, rsem, target):
        return pltpu.make_async_remote_copy(
            src_ref=src, dst_ref=dst, send_sem=ssem, recv_sem=rsem,
            device_id=target, device_id_type=MESH,
        )

    rows, cols = mc_ref.shape[1], mc_ref.shape[2]
    edge = pl.multiple_of((cols - 16) * o, 16)
    halo = []
    for dt in (-1, 0, 1):
        first = 0 if dt < 0 else rows - 2
        for ds in (0, 1):
            if (ds, dt) == (0, 0):
                continue
            k = len(halo)
            base = 3 * k
            sems = [(hs_sem.at[base + j], hr_sem.at[base + j]) for j in range(3)]
            target = dev(ds, None, dt)
            back = len(halo)
            copies = [
                (lat_ref, latx_ref.at[1 - dt, s]),
                (cl_ref, clx_ref.at[1 - dt, s]),
            ]
            if ds == 0:
                copies.append((mc_ref.at[:, pl.ds(first, 2)], mcv_ref.at[(1 - dt) // 2]))
            elif dt == 0:
                copies.append((mc_ref.at[:, :, pl.ds(edge, 16)], mch_ref.at[1]))
            else:
                copies.append(
                    (
                        mc_ref.at[:, pl.ds(first, 2), pl.ds(edge, 16)],
                        mch_ref.at[1 - dt, :, pl.ds(0, 2)],
                    )
                )
            halo.append(
                (
                    dt,
                    ds,
                    [remote(a, b, x, y, target) for (a, b), (x, y) in zip(copies, sems)],
                )
            )

    events = []
    for i in range(n - 1):
        for d in (0, 1):
            if d == 0:
                events.append((i, d, t - 1 - i, t - 1 - i >= 0))
            else:
                events.append((i, d, t + 1 + i, t + 1 + i <= n - 1))

    def begin_of(group, q):
        return (2 * (group % 4) + s) * per + q * span

    def block(group, part, q, u):
        begin = begin_of(group, q)
        if part == 0:
            return g_ref.at[u, pl.ds(begin, half)]
        if part == 1:
            return g_ref.at[u, pl.ds(begin + half, span - half)]
        return g_ref.at[u, pl.ds(begin, span)]

    tail = pl.ds(per * PIECES, rest)

    def z_copies(i, d, q, u, first):
        e = (2 * i + d) * PARTS + q
        target = dev(0, None, 1 if d == 0 else -1)
        src = w_ref.at[pl.ds(begin_of(g, q), span)] if first else block(g, 2, q, u)
        made = [remote(src, block(g, 2, q, u), zs_sem.at[2 * e], zr_sem.at[2 * e], target)]
        if q == PARTS - 1 and rest:
            src = w_ref.at[tail] if first else g_ref.at[u, tail]
            k = 2 * e + 1
            made.append(remote(src, g_ref.at[u, tail], zs_sem.at[k], zr_sem.at[k], target))
        return made

    def d_copies(e, q, u):
        def one(k, group, part, to):
            b = block(group, part, q, u)
            return remote(b, b, ps_sem.at[6 * e + k], pr_sem.at[6 * e + k], dev(0, to))

        first = [one(0, g, 0, gx), one(1, g, 1, gy)]
        second = [one(2, g, 0, gy), one(3, gx, 0, gy), one(4, g, 1, gx), one(5, gy, 1, gx)]
        return first, second

    def s_copies(e, q, u):
        plan = [(g, 2), (gx, 0), (gy, 1), (gy, 0), (gd, 0), (gx, 1), (gd, 1)]
        made = []
        for k, (group, part) in enumerate(plan):
            b = block(group, part, q, u)
            made.append(remote(b, b, ss_sem.at[7 * e + k], sr_sem.at[7 * e + k], dev(1)))
        return made

    def begin_z(i, d, q, u, valid, first):
        dt = 1 if d == 0 else -1

        def go():
            for copy in z_copies(i, d, q, u, first):
                copy.start()

        pl.when(jnp.logical_and(valid, has[dt]))(go)

    def end_z(i, d, q, u, valid):
        dt = 1 if d == 0 else -1

        def go():
            for copy in z_copies(i, d, q, u, i == 0):
                copy.wait_send()

        pl.when(jnp.logical_and(valid, has[dt]))(go)

    for q in range(PARTS):
        begin_z(0, 0, q, t, t >= 0, True)
        begin_z(0, 1, q, t, t >= 0, True)
    for dt, ds, copies in halo:
        def go(copies=copies):
            for copy in copies:
                copy.start()
        guarded(has[dt], go)

    def arrive(i, d, q, u):
        for copy in z_copies(i, d, q, u, False):
            copy.wait_recv()

    def stage_a(i, d, q, u, valid):
        e = (2 * i + d) * PARTS + q

        def go():
            arrive(i, d, q, u)
            if i + 1 < n - 1:
                begin_z(i + 1, d, q, u, valid, False)
            for copy in d_copies(e, q, u)[0]:
                copy.start()
            s_copies(e, q, u)[0].start()

        pl.when(valid)(go)

    def stage_b(i, d, q, u, valid):
        e = (2 * i + d) * PARTS + q

        def go():
            first, second = d_copies(e, q, u)
            sib = s_copies(e, q, u)
            first[0].wait_recv()
            second[0].start()
            second[1].start()
            sib[1].start()
            first[1].wait_recv()
            second[2].start()
            second[3].start()
            sib[2].start()

        pl.when(valid)(go)

    def stage_c(i, d, q, u, valid):
        e = (2 * i + d) * PARTS + q

        def go():
            _, second = d_copies(e, q, u)
            sib = s_copies(e, q, u)
            for k in range(4):
                second[k].wait_recv()
                sib[3 + k].start()

        pl.when(valid)(go)

    for slot in range((n - 1) * PARTS + 2):
        for stage, lag in ((stage_a, 0), (stage_b, 1), (stage_c, 2)):
            i, q = (slot - lag) // PARTS, (slot - lag) % PARTS
            if 0 <= i < n - 1:
                for _, d, u, valid in events[2 * i : 2 * i + 2]:
                    stage(i, d, q, u, valid)

    for copy in own:
        copy.wait()
    for dt, ds, copies in halo:
        guarded(has[dt], lambda copies=copies: [c.wait_send() for c in copies] and None)
    order = {(dt, ds): copies for dt, ds, copies in halo}
    for (dt, ds), copies in order.items():
        guarded(has[-dt], lambda copies=copies: [c.wait_recv() for c in copies] and None)
    for i, d, u, valid in events:
        for q in range(PARTS):
            e = (2 * i + d) * PARTS + q

            def finish(e=e, q=q, u=u):
                first, second = d_copies(e, q, u)
                for copy in first + second:
                    copy.wait_send()
                for copy in s_copies(e, q, u):
                    copy.wait()

            pl.when(valid)(finish)
            sent = t - i if d == 0 else t + i
            end_z(i, d, q, sent, sent >= 0 if d == 0 else sent <= n - 1)


def exchange(n, weights, latent, cache_latent, mid_cache):
    frames, rows, cols, channels = mid_cache.shape
    dt = weights.dtype
    shape = jax.ShapeDtypeStruct
    events = 2 * (n - 1) * PARTS
    dma = lambda k: pltpu.SemaphoreType.DMA((k,))
    return pl.pallas_call(
        functools.partial(exchange_kernel, n),
        out_shape=(
            shape((n,) + weights.shape, dt),
            shape((3, 2) + latent.shape, dt),
            shape((3, 2) + cache_latent.shape, dt),
            shape((2, frames, 2, cols, channels), dt),
            shape((3, frames, rows, 16, channels), dt),
        ),
        in_specs=[pl.BlockSpec(memory_space=pl.ANY)] * 4,
        out_specs=[pl.BlockSpec(memory_space=pl.ANY)] * 5,
        scratch_shapes=[
            dma(3), dma(15), dma(15), dma(2 * events), dma(2 * events),
            dma(6 * events), dma(6 * events), dma(7 * events), dma(7 * events),
        ],
        compiler_params=pltpu.CompilerParams(collective_id=0, has_side_effects=True),
    )(weights, latent, cache_latent, mid_cache)


def inside(start, count, limit):
    index = start + jnp.arange(count)
    return jnp.logical_and(index >= 0, index < limit)


def convs_kernel(
    beside_ref, taps_ref, gain_ref, cache_ref, region_ref, mask_ref, w_ref, u_ref, out_ref,
    x_ref, feat_ref, xs_ref, acc_ref, mx_ref, up_ref, tmp_ref,
):
    step = pl.program_id(0)
    total, tall, wide, mid = x_ref.shape
    frames, inner = total - 2, tall - 2
    rows = inner - 2
    cols = out_ref.shape[2] // 2
    out_channels = out_ref.shape[3]

    @pl.when(step == 0)
    def _():
        acc_ref[...] = jnp.zeros_like(acc_ref)
        x_ref[0 : total - frames] = cache_ref[...]
        size = tall * wide

        @pl.loop(0, frames)
        def _(f):
            value = jnp.zeros((size, mid), jnp.float32)
            for a in range(3):
                for b in range(3):
                    left = beside_ref[f + a, b : b + tall].reshape(size, beside_ref.shape[3])
                    value += jnp.dot(
                        left, taps_ref[3 * a + b], preferred_element_type=jnp.float32
                    )
            value = value.astype(jnp.bfloat16).astype(jnp.float32)
            moved = pltpu.roll(value, size - 1, axis=0).reshape(tall, wide, mid)
            feat_ref[f] = moved[1:-1].astype(jnp.bfloat16)
            power = jnp.mean(value * value, axis=-1, keepdims=True)
            value = value * lax.rsqrt(power + 1e-06) * gain_ref[...]
            value = jnp.where(region_ref[...] > 0, value / (1.0 + jnp.exp(-value)), 0.0)
            x_ref[total - frames + f] = value.astype(jnp.bfloat16).reshape(tall, wide, mid)

        @pl.loop(0, total)
        def _(f):
            value = x_ref[f].reshape(tall * wide, mid).astype(jnp.float32)
            for c in (1, 2):
                moved = pltpu.roll(value, tall * wide - c, axis=0)
                xs_ref[c - 1, f] = moved.astype(jnp.bfloat16).reshape(tall, wide, mid)

    @pl.when(step < 9)
    def _():
        a, b = step // 3, step % 3
        where = (pl.ds(a, frames), pl.ds(b, inner))
        size = frames * inner * wide
        left = [x_ref[where]] + [xs_ref[(c,) + where] for c in range(2)]
        left = jnp.concatenate([v.reshape(size, mid) for v in left], axis=1)
        weights = [
            jnp.concatenate([w_ref[u, c] for u in range(w_ref.shape[0])], axis=0)
            for c in range(3)
        ]
        acc_ref[...] += lax.dot_general(
            left, jnp.concatenate(weights, axis=1), (((1,), (1,)), ((), ())),
            preferred_element_type=jnp.float32,
        )

    @pl.when(step == 9)
    def _():
        up_ref[...] = jnp.zeros_like(up_ref)
        size = inner * wide

        @pl.loop(0, frames)
        def _(f):
            at = pl.ds(pl.multiple_of(f * size, size), size)
            value = acc_ref[at] + feat_ref[f].reshape(size, mid).astype(jnp.float32)
            value = jnp.where(mask_ref[...] > 0, value, 0.0)
            for c in range(3):
                moved = value if c == 0 else pltpu.roll(value, size - c, axis=0)
                mx_ref[c, f] = moved.astype(jnp.bfloat16).reshape(inner, wide, mid)

    @pl.when(step >= 9)
    def _():
        b = step - 9
        size = frames * rows * cols
        left = [mx_ref[c, :, pl.ds(b, rows), pl.ds(0, cols)] for c in range(3)]
        left = jnp.concatenate([v.reshape(size, mid) for v in left], axis=1)
        up_ref[...] += jnp.dot(
            left, u_ref[...].reshape(3 * mid, u_ref.shape[2]), preferred_element_type=jnp.float32
        )

    @pl.when(step == 11)
    def _():
        @pl.loop(0, frames * rows)
        def _(q):
            f, r = q // rows, q % rows
            value = up_ref[pl.ds(pl.multiple_of(q * cols, cols), cols)]
            value = jnp.concatenate([value, jnp.zeros((cols, 128), jnp.float32)], axis=1)
            for i in range(2):
                for j in range(2):
                    k = (2 * i + j) * out_channels
                    for h in range(tmp_ref.shape[0]):
                        part = value[:, k + 128 * h : k + 128 * h + 128]
                        tmp_ref[h, pl.ds(j, cols, stride=2), :] = part
                joined = jnp.concatenate([tmp_ref[h] for h in range(tmp_ref.shape[0])], axis=1)
                out_ref[f, 2 * r + i] = joined[:, :out_channels].astype(jnp.bfloat16)


def convs(beside, taps, gain, cache, region, mask, weights, up_weight, cols):
    total = beside.shape[0]
    tall, wide, mid = cache.shape[1:]
    frames, inner = total - 2, tall - 2
    rows = inner - 2
    phases = up_weight.shape[-1]
    whole = pl.BlockSpec(memory_space=pltpu.VMEM)
    flops = 2 * frames * wide * inner * 27 * mid * mid
    return pl.pallas_call(
        convs_kernel,
        grid=(12,),
        out_shape=jax.ShapeDtypeStruct((frames, 2 * rows, 2 * cols, phases // 4), jnp.bfloat16),
        in_specs=[
            whole,
            whole,
            whole,
            whole,
            whole,
            whole,
            pl.BlockSpec(
                (weights.shape[0], 3) + weights.shape[2:],
                lambda i: (0, jnp.minimum(i, 8), 0, 0),
            ),
            pl.BlockSpec((3, mid, phases), lambda i: (jnp.maximum(i - 9, 0), 0, 0)),
        ],
        out_specs=whole,
        scratch_shapes=[
            pltpu.VMEM((total, tall, wide, mid), jnp.bfloat16),
            pltpu.VMEM((frames, inner, wide, mid), jnp.bfloat16),
            pltpu.VMEM((2, total, tall, wide, mid), jnp.bfloat16),
            pltpu.VMEM((frames * inner * wide, mid), jnp.float32),
            pltpu.VMEM((3, frames, inner, wide, mid), jnp.bfloat16),
            pltpu.VMEM((frames * rows * cols, phases), jnp.float32),
            pltpu.VMEM((-(-phases // 512), 2 * cols, 128), jnp.float32),
        ],
        compiler_params=pltpu.CompilerParams(vmem_limit_bytes=48 * 2**20),
        cost_estimate=pl.CostEstimate(flops=flops, bytes_accessed=16 * 2**20, transcendentals=0),
    )(beside, taps, gain, cache, region, mask, weights, up_weight)


def local(
    n, latent, latent_mean, latent_scale, cache_latent, input_weight,
    mid_gain, mid_cache, mid_weight, up_weight,
):
    s = lax.axis_index("section")
    t = lax.axis_index("tile")
    channels = latent_mean.shape[0]
    mid = input_weight.shape[-1]
    cw = mid_weight.shape[-1]
    _, rows, cols, _ = mid_cache.shape[1:]
    shard = mid_weight.transpose(0, 1, 2, 4, 3).reshape(-1, 16 if cw % 16 == 0 else 8, mid)
    gathered, latx, clx, mcv, mch = exchange(
        n, shard, latent[0], cache_latent[0], mid_cache[0]
    )
    width = latx.shape[-1]
    frames = 2 * latx.shape[2]
    near = latx.transpose(1, 2, 0, 3, 4).reshape(frames, 3 * rows, width)[:, rows - 3 : 2 * rows + 3]
    repeats = width // channels
    scaled = (
        near.astype(jnp.float32) * jnp.tile(latent_scale, repeats) + jnp.tile(latent_mean, repeats)
    ).astype(jnp.bfloat16)
    cached = clx.transpose(2, 0, 3, 1, 4).reshape(clx.shape[2], 3 * rows, width)
    cached = cached[:, rows - 3 : 2 * rows + 3]
    joined = jnp.concatenate([cached, scaled], axis=0)
    joined = jnp.where(inside(t * rows - 3, rows + 6, n * rows)[:, None], joined, 0)
    joined = jnp.pad(joined, ((0, 0), (0, 0), (3 * channels, 3 * channels)))
    joined = lax.dynamic_slice_in_dim(joined, s * cols * channels, (cols + 6) * channels, axis=2)
    joined = joined.reshape(joined.shape[0], rows + 6, cols + 6, channels)
    wide = -(-(cols + 4) // 16) * 16
    extra = wide - cols - 4
    beside = jnp.concatenate([joined[:, :, c : c + cols + 4] for c in range(3)], axis=-1)
    beside = jnp.pad(beside, ((0, 0), (0, 0), (0, extra), (0, 0)))
    sided = jnp.concatenate([mch[0, :, :2], mch[1], mch[2, :, :2]], axis=1)
    sided = lax.dynamic_slice_in_dim(sided, 14 * s, 2, axis=2)
    centre = jnp.concatenate([mcv[0], mid_cache[0], mcv[1]], axis=1)
    cache = jnp.concatenate([sided, centre, sided], axis=2)
    row_ok = inside(t * rows - 2, rows + 4, n * rows)[:, None, None]
    col_ok = inside(s * cols - 2, cols + 4, 2 * cols)[:, None]
    region = jnp.logical_and(row_ok, col_ok)
    cache = jnp.pad(jnp.where(region, cache, 0), ((0, 0), (0, 0), (0, extra), (0, 0)))
    keep = jnp.pad(region[1:-1, 1:], ((0, 0), (0, extra + 1), (0, 0))).astype(jnp.float32)
    region = jnp.pad(region, ((0, 0), (0, extra), (0, 0))).astype(jnp.float32)
    out = convs(
        beside, input_weight.reshape(9, 3 * channels, mid), mid_gain[None], cache,
        region.reshape(-1, 1), keep.reshape(-1, 1), gathered.reshape(n, 27, cw, mid),
        up_weight.reshape((9,) + up_weight.shape[2:]), cols,
    )
    return out[None]


def solution(mesh):
    return jax.shard_map(
        functools.partial(local, mesh.shape["tile"]),
        mesh=mesh,
        in_specs=(
            P("grp", "section", "tile", None),
            P(),
            P(),
            P("grp", None, "tile", "section"),
            P(),
            P(),
            P("grp", None, "tile", "section", None),
            P(None, None, None, None, "tile"),
            P(),
        ),
        out_specs=P("grp", None, "tile", "section", None),
        check_vma=False,
    )
```
